32 devices in a mesh: patch: 8 (over y, x, core), vgroup: 4 (over z).
Axes of the slice: x: 2, y: 2, z: 4, core: 2. Of those that a mesh axis runs over, the one named last changes fastest.
Arguments:
- exposures: bfloat16 [4, 256, 62, 2048], P('vgroup', 'patch'), may hold values from -6 to 6
- target_patch: int32 [4, 256, 1], P('vgroup'), may hold values from 0 to 7; in each aligned block of 32 rows (0 to 31, 32 to 63, ..., all dimensions but the last counted through in order) at most 8 rows name the same one
- row_offset: int32 [4, 256], P('vgroup'), may hold values from 0 to 224
- basis_index: int32 [4, 256, 3], P('vgroup'), may hold values from 0 to 34
- basis_coef: float32 [4, 256, 3], P('vgroup'), may hold values from 0.3 to 1.5
- inv_variance: float32 [4, 256], P('vgroup'), may hold values from 0.25 to 4
- psf_basis: float32 [35, 2, 31], replicated, may hold values from -1 to 1
Outputs:
- coadd: float32 [2048, 2048], P(('patch', 'vgroup'))
- weight_map: float32 [2048], P(('patch', 'vgroup'))
The draws below stay inside these ranges and needn't reach their ends.
Inputs may be any that keep to these rules, and one draw needn't show every extreme that they name: `target_patch`: among the 32 blocks of one device (aligned blocks along the second dimension), at most 8 name the same patch, a bound that some block reaches of them.
All inputs are finite; a program needn't handle non-finite values.
Results may differ from the reference program's by a relative error of at most 0.003.
Values may be sent and summed in bfloat16 or wider, within the bound.
A program may use at most 128 MiB of HBM per device.

```python
import math
import jax
import jax.numpy as jnp
import numpy as np
from jax import lax

W = 2048
BR = 32
HALO = 15
KTAP = 31
NBASIS = 35
NT = 3
NB_DEV = 32
PR = 256
CAP = 8
BLOCKS = 256
N_PATCH = 8
N_VGROUP = 4


def set_ends(values, key, least, high):
    place = [jax.random.randint(jax.random.fold_in(key, axis), (), 0, length) for axis, length in enumerate(values.shape)]
    main_axis = values.shape.index(max(values.shape))
    neighbour = place[:main_axis] + [(place[main_axis] + 1) % values.shape[main_axis]] + place[main_axis + 1:]
    return values.at[tuple(place)].set(least).at[tuple(neighbour)].set(high)


def levels(stream_key, dims, shards, low, largest):
    def one(dim, shards_of):
        steps = jax.random.uniform(jax.random.fold_in(jax.random.fold_in(stream_key, 6), dim), (shards_of,), jnp.float32, low / len(shards), largest / len(shards))
        return jnp.repeat(jnp.exp(steps), dims[dim] // shards_of).reshape((-1,) + (1,) * (len(dims) - dim - 1))

    gain = one(*shards[0])
    for cut in shards[1:]:
        gain = gain * one(*cut)
    return gain


def routed_block(stream_key, own, number, rows, amount, top, bound, skew):
    order = jax.random.permutation(stream_key, amount)
    heavy_load, usual = portions_of(amount, rows * top, bound, skew, True), portions_of(amount, rows * top, bound, skew, False)
    places = jnp.arange(amount)

    def named(lengths, turn):
        used = int((lengths > 0).sum())
        fixed = max(1, used // 4)
        shifted = fixed + (places - fixed + turn * (used - fixed)) % max(1, amount - fixed)
        return jnp.zeros((amount,), jnp.int32).at[order[jnp.where(places < fixed, places, shifted)]].set(jnp.asarray(lengths, jnp.int32))

    lengths = jnp.where(number % 4 == 0, named(heavy_load, number // 4), named(usual, number - number // 4 - 1))
    mixed = jax.random.permutation(jax.random.fold_in(own, 3), amount)
    giver, sink = mixed[0:amount // 2 * 2:2], mixed[1:amount // 2 * 2:2]
    margin = jnp.minimum(lengths[giver] - 1, bound - lengths[sink]) // 2
    margin = jnp.where((giver == order[0]) | (sink == order[0]) | (lengths[sink] == 0), 0, jnp.maximum(margin, 0))
    shifted = jax.random.randint(jax.random.fold_in(own, 4), (amount // 2,), 0, 1 << 20) % (margin + 1)
    lengths = lengths.at[giver].add(-shifted).at[sink].add(shifted)
    labels = jnp.searchsorted(jnp.cumsum(lengths), jnp.arange(rows * top), side="right").astype(jnp.int32)
    listing = labels.reshape(top, rows).T
    listing = listing[jax.random.permutation(jax.random.fold_in(own, 1), rows)]
    turn = jax.random.randint(jax.random.fold_in(own, 2), (rows, 1), 0, top)
    return jnp.take_along_axis(listing, (jnp.arange(top)[None, :] + turn) % top, axis=1)


def portions_of(amount, total, most, lean, full):
    portions = [(1 << 20) // math.isqrt(rank ** lean) + 1 for rank in range(1, amount + 1)]
    largest = most if full else min(most, max(-(-total // amount), total * portions[0] // sum(portions)))
    least = 1 if total - largest >= amount - 1 else 0
    given, spare = [largest] + [least] * (amount - 1), total - largest - least * (amount - 1)
    while spare > 0:
        candidates = [i for i in range(1, amount) if given[i] < largest] or [i for i in range(1, amount) if given[i] < most]
        pool, remaining = sum([portions[i] for i in candidates]), spare
        for i in candidates:
            more = min(most - given[i], max(1, remaining * portions[i] // pool), spare)
            given[i] = given[i] + more
            spare = spare - more
    return np.array(given)


def bell_draw(own_key, dims, scale, reach, cuts=(), kind=jnp.bfloat16):
    array = scale * jax.random.normal(own_key, dims, jnp.float32)
    if cuts:
        array = array * levels(own_key, dims, cuts, -0.22, 0.18)
    return jnp.clip(array, -reach, reach).astype(kind)


def setup_inputs(seed: int = 0) -> dict:
    seeds = jax.random.split(jax.random.key(seed), 8)
    exposures = bell_draw(seeds[0], (N_VGROUP, BLOCKS, BR + 2 * HALO, W), 1.0, 6.0, ((0, 4), (1, 8)))
    target_patch_keys = jax.random.split(jax.random.fold_in(seeds[1], 1), N_VGROUP * BLOCKS // NB_DEV)
    target_patch_turns = jax.random.permutation(jax.random.fold_in(seeds[1], 3), N_VGROUP * BLOCKS // NB_DEV)
    target_patch = jax.vmap(lambda own, number: routed_block(jax.random.fold_in(seeds[1], 2), own, number, NB_DEV, N_PATCH, 1, CAP, 1))(target_patch_keys, target_patch_turns).reshape((N_VGROUP, BLOCKS, 1))
    row_offset = set_ends(jax.random.randint(seeds[2], (N_VGROUP, BLOCKS), 0, PR - BR + 1), jax.random.fold_in(seeds[2], 1), 0, PR - BR).astype(jnp.int32)
    basis_index = set_ends(jax.random.randint(seeds[3], (N_VGROUP, BLOCKS, NT), 0, NBASIS), jax.random.fold_in(seeds[3], 1), 0, NBASIS - 1).astype(jnp.int32)
    basis_coef = jnp.clip(0.3 + 1.2 * jax.random.uniform(seeds[4], (N_VGROUP, BLOCKS, NT), jnp.float32) ** levels(seeds[4], (N_VGROUP, BLOCKS, NT), ((0, 4),), -0.2, 0.2), 0.3, 1.5)
    inv_variance = jnp.clip(jnp.exp(math.log(4.0) - 2.7725887 * jax.random.uniform(seeds[5], (N_VGROUP, BLOCKS), jnp.float32) ** levels(seeds[5], (N_VGROUP, BLOCKS), ((0, 4),), -0.2, 0.2)), 0.25, 4.0)
    psf_basis = bell_draw(seeds[6], (NBASIS, 2, KTAP), 0.18, 1.0, (), jnp.float32)
    return {"exposures": exposures, "target_patch": target_patch, "row_offset": row_offset, "basis_index": basis_index, "basis_coef": basis_coef, "inv_variance": inv_variance, "psf_basis": psf_basis}


def psf_match(blocks, kernel_taps, coefficient):
    halo_rows = (kernel_taps.shape[-1] - 1) // 2
    columns = blocks.shape[-1]
    out_rows = blocks.shape[-2] - 2 * halo_rows
    pixels = blocks.astype(jnp.float32)
    padded = jnp.pad(pixels, [(0, 0)] * (pixels.ndim - 1) + [(halo_rows, halo_rows)])
    summed = jnp.zeros(pixels.shape[:-2] + (out_rows, columns), jnp.float32)
    for term_id in range(kernel_taps.shape[-3]):
        across = jnp.zeros_like(pixels)
        for tap_id in range(kernel_taps.shape[-1]):
            across = across + kernel_taps[..., term_id, 1, tap_id, None, None] * padded[..., :, tap_id:tap_id + columns]
        downward = jnp.zeros_like(summed)
        for tap_id in range(kernel_taps.shape[-1]):
            downward = downward + kernel_taps[..., term_id, 0, tap_id, None, None] * across[..., tap_id:tap_id + out_rows, :]
        summed = summed + coefficient[..., term_id, None, None] * downward
    return summed.astype(jnp.bfloat16)


def reference(exposures, target_patch, row_offset, basis_index, basis_coef, inv_variance, psf_basis):
    numerator = jnp.zeros((N_PATCH * PR, W), jnp.float32)
    weight_sum = jnp.zeros((N_PATCH * PR,), jnp.float32)

    def visit_group(running, inputs):
        numer_acc, weight_acc = running
        blocks, targets, offsets, indices, coefs, inverse = inputs
        kernel_taps = psf_basis[indices]
        matched = lax.map(lambda members: psf_match(*members),
                          (blocks.reshape(N_PATCH, NB_DEV, BR + 2 * HALO, W),
                           kernel_taps.reshape(N_PATCH, NB_DEV, NT, 2, KTAP),
                           coefs.reshape(N_PATCH, NB_DEV, NT)))
        matched = matched.reshape(N_PATCH * NB_DEV, BR, W)
        row_index = (targets[:, 0] * PR + offsets)[:, None] + jnp.arange(BR, dtype=jnp.int32)[None, :]
        numer_acc = numer_acc.at[row_index].add(inverse[:, None, None] * matched.astype(jnp.float32))
        weight_acc = weight_acc.at[row_index].add(jnp.broadcast_to(inverse[:, None], row_index.shape))
        return (numer_acc, weight_acc), None

    (numer_acc, weight_acc), _ = lax.scan(visit_group, (numerator, weight_sum),
                                          (exposures, target_patch, row_offset, basis_index, basis_coef, inv_variance))
    return numer_acc / (1.0 + weight_acc[:, None]), weight_acc
```

```python
import functools

import jax
import jax.numpy as jnp
from jax import lax
from jax.experimental import pallas as pl
from jax.experimental.pallas import tpu as pltpu
from jax.sharding import PartitionSpec as P

PR = 256
LANES = 128
DENSE_LIMIT = 24 * 1024 * 1024
VMEM_LIMIT = 60 * 1024 * 1024


def split_bf16(values):
    high = values.astype(jnp.bfloat16)
    low = (values - high.astype(jnp.float32)).astype(jnp.bfloat16)
    return high, low


def build_tables(basis_ref, down_table, across_table, n_basis, taps):
    half = (taps - 1) // 2
    first = LANES // 2 - half

    def build(b, carry):
        line = basis_ref[b]
        down = pltpu.roll(
            jnp.broadcast_to(line[0:1, :], (32, LANES)), 0, 1, stride=1, stride_axis=0
        )
        down_table[b] = down
        reverse = jnp.broadcast_to(line[1:2, :], (2 * LANES, LANES))
        band = pltpu.roll(reverse, 0, 1, stride=1, stride_axis=0)
        tap = (
            lax.broadcasted_iota(jnp.int32, band.shape, 0)
            - lax.broadcasted_iota(jnp.int32, band.shape, 1)
            - first
        )
        band = jnp.where(jnp.logical_and(tap >= 0, tap < taps), band, 0.0)
        high, low = split_bf16(band)
        across_table[b, :, 0:LANES] = high
        across_table[b, :, LANES : 2 * LANES] = low
        return carry

    lax.fori_loop(0, n_basis, build, 0)


def match_block(b, index_ref, coef_ref, blocks_ref, pixels, windows, down_table, across_table, n_terms):
    in_rows, columns = blocks_ref.shape[1:]
    tiles = columns // LANES
    block = blocks_ref[b]
    pixels[0:in_rows, :] = block
    pixels[64 : 64 + in_rows, :] = block
    picks = [index_ref[b * n_terms + t] for t in range(n_terms)]
    rows = jnp.concatenate(
        [coef_ref[b * n_terms + t] * down_table[picks[t]] for t in range(n_terms)], axis=0
    )
    rows_high = rows.astype(jnp.bfloat16).astype(jnp.float32)
    lane = lax.broadcasted_iota(jnp.int32, rows.shape, 1)
    taps_down = jnp.where(lane < 64, rows_high, rows - rows_high).astype(jnp.bfloat16)
    for q in range(0, tiles, 2):
        down = jnp.dot(
            taps_down,
            pixels[:, q * LANES : (q + 2) * LANES],
            preferred_element_type=jnp.float32,
        )
        high, low = split_bf16(down)
        for t in range(n_terms):
            for h in range(2):
                for part, offset in ((high, 0), (low, 32)):
                    tile = part[t * 32 : t * 32 + 32, h * LANES : (h + 1) * LANES]
                    right = (q + h) * 64 + offset
                    windows[right : right + 32, (2 * t + 1) * LANES : (2 * t + 2) * LANES] = tile
                    windows[right + 64 : right + 96, 2 * t * LANES : (2 * t + 1) * LANES] = tile
    taps_across = jnp.concatenate([across_table[picks[t]] for t in range(n_terms)], axis=0)
    product = jnp.dot(windows[...], taps_across, preferred_element_type=jnp.float32)
    product = product[:, 0:LANES] + product[:, LANES : 2 * LANES]
    out = [product[c * 64 : c * 64 + 32] + product[c * 64 + 32 : c * 64 + 64] for c in range(tiles + 1)]
    lane = lax.broadcasted_iota(jnp.int32, out[0].shape, 1)
    out[0] = jnp.where(lane < LANES // 2, out[tiles], out[0])
    return jnp.concatenate(out[:tiles], axis=1).astype(jnp.bfloat16)


def match_kernel(
    dense, n_terms, taps,
    index_ref, coef_ref, start_ref, inverse_ref, blocks_ref, basis_ref, out_ref,
    pixels, windows, down_table, across_table,
):
    count = blocks_ref.shape[0]
    build_tables(basis_ref, down_table, across_table, basis_ref.shape[0], taps)
    pixels[...] = jnp.zeros_like(pixels)
    windows[...] = jnp.zeros_like(windows)
    if dense:
        out_ref[...] = jnp.zeros_like(out_ref)

    def body(step, carry):
        for k in range(2):
            b = step * 2 + k
            matched = match_block(
                b, index_ref, coef_ref, blocks_ref, pixels.at[k], windows.at[k],
                down_table, across_table, n_terms,
            )
            if dense:
                start = start_ref[b]
                first = jnp.minimum((start // 8) * 8, out_ref.shape[0] - 40)
                row = lax.broadcasted_iota(jnp.int32, (40, 32), 0)
                column = lax.broadcasted_iota(jnp.int32, (40, 32), 1)
                place = (row - column == start - first).astype(jnp.float32).astype(jnp.bfloat16)
                shifted = jnp.dot(place, matched, preferred_element_type=jnp.float32)
                out_ref[pl.ds(pl.multiple_of(first, 8), 40), :] += inverse_ref[b] * shifted
            else:
                out_ref[b] = matched
        return carry

    lax.fori_loop(0, count // 2, body, 0)


def match_all(blocks, picks, coef, starts, inverse, psf_basis, n_patch, dense):
    count, in_rows, columns = blocks.shape
    n_basis, _, taps = psf_basis.shape
    n_terms = picks.shape[0] // count
    half = (taps - 1) // 2
    tiles = columns // LANES
    down_line = jnp.pad(psf_basis[:, 0], ((0, 0), (0, 64 - taps)))
    down_line = jnp.concatenate([down_line, down_line], axis=1)
    tail = LANES - (LANES // 2 - half) - taps + 1
    across_line = jnp.pad(psf_basis[:, 1, ::-1], ((0, 0), (tail, LANES - taps - tail)))
    lines = jnp.stack([down_line, across_line], axis=1)
    if dense:
        out = jax.ShapeDtypeStruct((n_patch * PR, columns), jnp.float32)
    else:
        out = jax.ShapeDtypeStruct((count, in_rows - taps + 1, columns), jnp.bfloat16)
    smem = pl.BlockSpec(memory_space=pltpu.SMEM)
    vmem = pl.BlockSpec(memory_space=pltpu.VMEM)
    return pl.pallas_call(
        functools.partial(match_kernel, dense, n_terms, taps),
        out_shape=out,
        in_specs=[smem] * 4 + [vmem] * 2,
        out_specs=vmem,
        scratch_shapes=[
            pltpu.VMEM((2, 128, columns), jnp.bfloat16),
            pltpu.VMEM((2, (tiles + 1) * 64, n_terms * 2 * LANES), jnp.bfloat16),
            pltpu.VMEM((n_basis, 32, LANES), jnp.float32),
            pltpu.VMEM((n_basis, 2 * LANES, 2 * LANES), jnp.bfloat16),
        ],
        compiler_params=pltpu.CompilerParams(vmem_limit_bytes=VMEM_LIMIT),
    )(picks, coef, starts, inverse, blocks, lines)


def slots_route(matched, own_target, targets, row_offset, inverse, n_patch, own_patch):
    per_device = matched.shape[0]
    capacity = 2 * per_device // n_patch
    out_rows = matched.shape[1]
    positions = jnp.arange(per_device, dtype=jnp.int32)
    same_patch = targets[:, :, None] == targets[:, None, :]
    earlier = positions[None, :, None] > positions[None, None, :]
    slot_rank = jnp.sum(jnp.logical_and(same_patch, earlier), axis=2)
    peer_ids = jnp.arange(n_patch, dtype=jnp.int32)
    slot_ids = jnp.arange(capacity, dtype=jnp.int32)
    own_rank = lax.dynamic_slice_in_dim(slot_rank, own_patch, 1, 0)[0]
    source_pick = jnp.logical_and(
        own_target[None, None, :] == peer_ids[:, None, None],
        own_rank[None, None, :] == slot_ids[None, :, None],
    )
    source_index = jnp.sum(source_pick * positions[None, None, :], axis=2)
    present = jnp.any(source_pick, axis=2).astype(jnp.bfloat16)[:, :, None, None]
    taking = jnp.logical_and(
        targets[:, None, :] == own_patch, slot_rank[:, None, :] == slot_ids[None, :, None]
    )
    offsets_in = jnp.sum(taking * row_offset.reshape(n_patch, 1, per_device), axis=2)
    weights_in = jnp.sum(taking * inverse.reshape(n_patch, 1, per_device), axis=2)
    outgoing = matched[source_index] * present
    arrived = lax.all_to_all(outgoing, "patch", split_axis=0, concat_axis=0, tiled=True)
    slot_count = n_patch * capacity
    matched = arrived.reshape((slot_count,) + arrived.shape[2:])
    row_index = (
        offsets_in.reshape(slot_count)[:, None] + jnp.arange(out_rows, dtype=jnp.int32)[None, :]
    )
    placement = (row_index[None, :, :] == jnp.arange(PR, dtype=jnp.int32)[:, None, None]).astype(
        jnp.float32
    )
    placement = placement * weights_in.reshape(slot_count)[None, :, None]
    numerator = jnp.einsum(
        "rsi,siw->rw", placement, matched.astype(jnp.float32), precision=lax.Precision.HIGHEST
    )
    return lax.psum_scatter(numerator, "vgroup", scatter_dimension=0, tiled=True)


def swap_sum(keep, send, axis_name, pairs):
    got = lax.ppermute(send.astype(jnp.bfloat16), axis_name, pairs)
    return keep + got.astype(jnp.float32)


def dense_route(dense, own_patch, own_group, n_patch, n_group):
    columns = dense.shape[-1]
    sums = dense.reshape(n_patch, PR, columns)

    def flip(bit):
        return [(i, i ^ bit) for i in range(n_patch)]

    def cut(values, position, bit):
        mine = (own_patch // bit) % 2
        keep = lax.dynamic_index_in_dim(values, mine, position, keepdims=False)
        send = lax.dynamic_index_in_dim(values, 1 - mine, position, keepdims=False)
        return swap_sum(keep, send, "patch", flip(bit))

    sums = cut(sums.reshape(2, 2, 2, PR, columns), 2, 1)
    one = cut(cut(sums[:, :, : PR // 2], 1, 2), 0, 4)
    two = cut(cut(sums[:, :, PR // 2 :], 0, 4), 0, 2)
    sums = jnp.concatenate([one, two], axis=0).reshape(n_group, PR // n_group, columns)
    total = lax.dynamic_index_in_dim(sums, own_group, 0, keepdims=False)
    for shift in range(1, n_group):
        pairs = [(i, (i + shift) % n_group) for i in range(n_group)]
        send = lax.dynamic_index_in_dim(sums, (own_group + shift) % n_group, 0, keepdims=False)
        total = swap_sum(total, send, "vgroup", pairs)
    return total


def local(exposures, target_patch, row_offset, basis_index, basis_coef, inv_variance, psf_basis):
    n_patch, n_group = lax.axis_size("patch"), lax.axis_size("vgroup")
    own_patch, own_group = lax.axis_index("patch"), lax.axis_index("vgroup")
    blocks = exposures[0]
    per_device, in_rows, columns = blocks.shape
    taps = psf_basis.shape[-1]
    out_rows = in_rows - taps + 1
    share = PR // n_group
    dense = n_patch == 8 and n_patch * PR * columns * 4 <= DENSE_LIMIT

    def own(values):
        return lax.dynamic_slice_in_dim(values, own_patch * per_device, per_device, 0)

    all_starts = target_patch[0, :, 0] * PR + row_offset[0]
    starts, inverse = own(all_starts), own(inv_variance[0])
    picks, coef = own(basis_index[0]).reshape(-1), own(basis_coef[0]).reshape(-1)

    spread = jnp.stack([all_starts.astype(jnp.float32), inv_variance[0]])
    spread = lax.all_gather(spread, "vgroup", axis=0, tiled=False)
    first = own_patch * PR + own_group * share
    rows = (first + jnp.arange(share, dtype=jnp.int32)).astype(jnp.float32)[:, None, None]
    inside = jnp.logical_and(rows >= spread[None, :, 0], rows < spread[None, :, 0] + out_rows)
    weight = jnp.sum(jnp.where(inside, spread[None, :, 1], 0.0), axis=(1, 2))

    result = match_all(blocks, picks, coef, starts, inverse, psf_basis, n_patch, dense)
    if dense:
        numerator = dense_route(result, own_patch, own_group, n_patch, n_group)
    else:
        targets = target_patch[0, :, 0].reshape(n_patch, per_device)
        own_target = lax.dynamic_slice_in_dim(targets, own_patch, 1, 0)[0]
        numerator = slots_route(
            result, own_target, targets, row_offset[0], inv_variance[0], n_patch, own_patch
        )
    coadd = jnp.roll(numerator / (1.0 + weight[:, None]), -(LANES // 2), axis=1)
    return (coadd, weight)


def solution(mesh):
    in_specs = (
        P("vgroup", "patch", None, None),
        P("vgroup", None, None),
        P("vgroup", None),
        P("vgroup", None, None),
        P("vgroup", None, None),
        P("vgroup", None),
        P(),
    )
    out_specs = (P(("patch", "vgroup"), None), P(("patch", "vgroup")))
    return jax.shard_map(local, mesh=mesh, in_specs=in_specs, out_specs=out_specs, check_vma=False)
```

```python
import functools

import jax
import jax.numpy as jnp
from jax import lax
from jax.experimental import pallas as pl
from jax.experimental.pallas import tpu as pltpu
from jax.sharding import PartitionSpec as P

PR = 256
LANES = 128
DENSE_LIMIT = 24 * 1024 * 1024
VMEM_LIMIT = 60 * 1024 * 1024


def split_bf16(values):
    high = values.astype(jnp.bfloat16)
    low = (values - high.astype(jnp.float32)).astype(jnp.bfloat16)
    return high, low


def build_tables(basis_ref, down_table, across_table, n_basis, taps):
    half = (taps - 1) // 2
    first = LANES // 2 - half

    def build(b, carry):
        line = basis_ref[b]
        down = pltpu.roll(
            jnp.broadcast_to(line[0:1, :], (32, LANES)), 0, 1, stride=1, stride_axis=0
        )
        down_table[b] = down
        reverse = jnp.broadcast_to(line[1:2, :], (2 * LANES, LANES))
        band = pltpu.roll(reverse, 0, 1, stride=1, stride_axis=0)
        tap = (
            lax.broadcasted_iota(jnp.int32, band.shape, 0)
            - lax.broadcasted_iota(jnp.int32, band.shape, 1)
            - first
        )
        band = jnp.where(jnp.logical_and(tap >= 0, tap < taps), band, 0.0)
        high, low = split_bf16(band)
        across_table[b, :, 0:LANES] = high
        across_table[b, :, LANES : 2 * LANES] = low
        return carry

    lax.fori_loop(0, n_basis, build, 0)


def match_block(b, index_ref, coef_ref, blocks_ref, pixels, windows, down_table, across_table, n_terms):
    in_rows, columns = blocks_ref.shape[1:]
    tiles = columns // LANES
    block = blocks_ref[b]
    pixels[0:in_rows, :] = block
    pixels[64 : 64 + in_rows, :] = block
    picks = [index_ref[b * n_terms + t] for t in range(n_terms)]
    rows = jnp.concatenate(
        [coef_ref[b * n_terms + t] * down_table[picks[t]] for t in range(n_terms)], axis=0
    )
    rows_high = rows.astype(jnp.bfloat16).astype(jnp.float32)
    lane = lax.broadcasted_iota(jnp.int32, rows.shape, 1)
    taps_down = jnp.where(lane < 64, rows_high, rows - rows_high).astype(jnp.bfloat16)
    for q in range(0, tiles, 2):
        down = jnp.dot(
            taps_down,
            pixels[:, q * LANES : (q + 2) * LANES],
            preferred_element_type=jnp.float32,
        )
        high, low = split_bf16(down)
        for t in range(n_terms):
            for h in range(2):
                for part, offset in ((high, 0), (low, 32)):
                    tile = part[t * 32 : t * 32 + 32, h * LANES : (h + 1) * LANES]
                    right = (q + h) * 64 + offset
                    windows[right : right + 32, (2 * t + 1) * LANES : (2 * t + 2) * LANES] = tile
                    windows[right + 64 : right + 96, 2 * t * LANES : (2 * t + 1) * LANES] = tile
    taps_across = jnp.concatenate([across_table[picks[t]] for t in range(n_terms)], axis=0)
    product = jnp.dot(windows[...], taps_across, preferred_element_type=jnp.float32)
    product = product[:, 0:LANES] + product[:, LANES : 2 * LANES]
    out = [product[c * 64 : c * 64 + 32] + product[c * 64 + 32 : c * 64 + 64] for c in range(tiles + 1)]
    lane = lax.broadcasted_iota(jnp.int32, out[0].shape, 1)
    out[0] = jnp.where(lane < LANES // 2, out[tiles], out[0])
    return jnp.concatenate(out[:tiles], axis=1).astype(jnp.bfloat16)


def match_kernel(
    dense, n_terms, taps,
    index_ref, coef_ref, start_ref, inverse_ref, blocks_ref, basis_ref, out_ref,
    pixels, windows, down_table, across_table,
):
    count = blocks_ref.shape[0]
    build_tables(basis_ref, down_table, across_table, basis_ref.shape[0], taps)
    pixels[...] = jnp.zeros_like(pixels)
    windows[...] = jnp.zeros_like(windows)
    if dense:
        out_ref[...] = jnp.zeros_like(out_ref)

    def body(step, carry):
        for k in range(2):
            b = step * 2 + k
            matched = match_block(
                b, index_ref, coef_ref, blocks_ref, pixels.at[k], windows.at[k],
                down_table, across_table, n_terms,
            )
            if dense:
                start = start_ref[b]
                first = jnp.minimum((start // 8) * 8, out_ref.shape[0] - 40)
                row = lax.broadcasted_iota(jnp.int32, (40, 32), 0)
                column = lax.broadcasted_iota(jnp.int32, (40, 32), 1)
                place = (row - column == start - first).astype(jnp.float32).astype(jnp.bfloat16)
                shifted = jnp.dot(place, matched, preferred_element_type=jnp.float32)
                out_ref[pl.ds(pl.multiple_of(first, 8), 40), :] += inverse_ref[b] * shifted
            else:
                out_ref[b] = matched
        return carry

    lax.fori_loop(0, count // 2, body, 0)


def match_all(blocks, picks, coef, starts, inverse, psf_basis, n_patch, dense):
    count, in_rows, columns = blocks.shape
    n_basis, _, taps = psf_basis.shape
    n_terms = picks.shape[0] // count
    half = (taps - 1) // 2
    tiles = columns // LANES
    down_line = jnp.pad(psf_basis[:, 0], ((0, 0), (0, 64 - taps)))
    down_line = jnp.concatenate([down_line, down_line], axis=1)
    tail = LANES - (LANES // 2 - half) - taps + 1
    across_line = jnp.pad(psf_basis[:, 1, ::-1], ((0, 0), (tail, LANES - taps - tail)))
    lines = jnp.stack([down_line, across_line], axis=1)
    if dense:
        out = jax.ShapeDtypeStruct((n_patch * PR, columns), jnp.float32)
    else:
        out = jax.ShapeDtypeStruct((count, in_rows - taps + 1, columns), jnp.bfloat16)
    smem = pl.BlockSpec(memory_space=pltpu.SMEM)
    vmem = pl.BlockSpec(memory_space=pltpu.VMEM)
    return pl.pallas_call(
        functools.partial(match_kernel, dense, n_terms, taps),
        out_shape=out,
        in_specs=[smem] * 4 + [vmem] * 2,
        out_specs=vmem,
        scratch_shapes=[
            pltpu.VMEM((2, 128, columns), jnp.bfloat16),
            pltpu.VMEM((2, (tiles + 1) * 64, n_terms * 2 * LANES), jnp.bfloat16),
            pltpu.VMEM((n_basis, 32, LANES), jnp.float32),
            pltpu.VMEM((n_basis, 2 * LANES, 2 * LANES), jnp.bfloat16),
        ],
        compiler_params=pltpu.CompilerParams(vmem_limit_bytes=VMEM_LIMIT),
    )(picks, coef, starts, inverse, blocks, lines)


def slots_route(matched, own_target, targets, row_offset, inverse, n_patch, own_patch):
    per_device = matched.shape[0]
    capacity = 2 * per_device // n_patch
    out_rows = matched.shape[1]
    positions = jnp.arange(per_device, dtype=jnp.int32)
    same_patch = targets[:, :, None] == targets[:, None, :]
    earlier = positions[None, :, None] > positions[None, None, :]
    slot_rank = jnp.sum(jnp.logical_and(same_patch, earlier), axis=2)
    peer_ids = jnp.arange(n_patch, dtype=jnp.int32)
    slot_ids = jnp.arange(capacity, dtype=jnp.int32)
    own_rank = lax.dynamic_slice_in_dim(slot_rank, own_patch, 1, 0)[0]
    source_pick = jnp.logical_and(
        own_target[None, None, :] == peer_ids[:, None, None],
        own_rank[None, None, :] == slot_ids[None, :, None],
    )
    source_index = jnp.sum(source_pick * positions[None, None, :], axis=2)
    present = jnp.any(source_pick, axis=2).astype(jnp.bfloat16)[:, :, None, None]
    taking = jnp.logical_and(
        targets[:, None, :] == own_patch, slot_rank[:, None, :] == slot_ids[None, :, None]
    )
    offsets_in = jnp.sum(taking * row_offset.reshape(n_patch, 1, per_device), axis=2)
    weights_in = jnp.sum(taking * inverse.reshape(n_patch, 1, per_device), axis=2)
    outgoing = matched[source_index] * present
    arrived = lax.all_to_all(outgoing, "patch", split_axis=0, concat_axis=0, tiled=True)
    slot_count = n_patch * capacity
    matched = arrived.reshape((slot_count,) + arrived.shape[2:])
    row_index = (
        offsets_in.reshape(slot_count)[:, None] + jnp.arange(out_rows, dtype=jnp.int32)[None, :]
    )
    placement = (row_index[None, :, :] == jnp.arange(PR, dtype=jnp.int32)[:, None, None]).astype(
        jnp.float32
    )
    placement = placement * weights_in.reshape(slot_count)[None, :, None]
    numerator = jnp.einsum(
        "rsi,siw->rw", placement, matched.astype(jnp.float32), precision=lax.Precision.HIGHEST
    )
    return lax.psum_scatter(numerator, "vgroup", scatter_dimension=0, tiled=True)


def route_kernel(
    chunks, dense_ref, weight_ref, total_ref, weight_out_ref,
    send_core, got_core, send_one, got_one, keep_one, send_two, got_two, keep_two,
    send_group, got_group, got_weight,
    core_sems, one_sems, two_sems, group_sems, weight_sems,
):
    p, z = lax.axis_index("patch"), lax.axis_index("vgroup")
    n_group = dense_ref.shape[3]
    half = n_group // 2
    width = dense_ref.shape[-1] // chunks
    y, x, c = p // 4, (p // 2) % 2, p % 2
    across_core = (p + 1 - 2 * c, z)
    across_x = (p + 2 - 4 * x, z)
    across_y = (p + 4 - 8 * y, z)
    groups = [(z + d) % n_group for d in range(1, n_group)]
    across_z = [(p, to) for to in groups]

    barrier = pltpu.get_barrier_semaphore()
    partners = [across_core, across_x, across_y] + across_z
    for partner in partners:
        pl.semaphore_signal(barrier, inc=1, device_id=partner, device_id_type=pl.DeviceIdType.MESH)
    pl.semaphore_wait(barrier, len(partners))

    copies = []

    def go(source, target, sems, place, device):
        copy = pltpu.make_async_remote_copy(
            src_ref=source, dst_ref=target,
            send_sem=sems.at[(0,) + place], recv_sem=sems.at[(1,) + place],
            device_id=device, device_id_type=pl.DeviceIdType.MESH,
        )
        copy.start()
        copies.append(copy)
        return copy

    def wide(values):
        return values.astype(jnp.float32)

    core_copies, one_copies, two_copies, group_copies = {}, {}, {}, {}

    def stage_core(g):
        cols = slice(g * width, (g + 1) * width)
        send_core[g] = dense_ref[:, :, 1 - c, :, :, cols].astype(jnp.bfloat16)
        core_copies[g] = go(send_core.at[g], got_core.at[g], core_sems, (g,), across_core)

    def stage_one(g):
        cols = slice(g * width, (g + 1) * width)
        core_copies[g].wait_recv()
        low, high = slice(0, half), slice(half, n_group)
        send_one[g, 0] = (
            dense_ref[:, 1 - x, c, low, :, cols] + wide(got_core[g, :, 1 - x, low])
        ).astype(jnp.bfloat16)
        first = go(send_one.at[g, 0], got_one.at[g, 0], one_sems, (g, 0), across_x)
        send_one[g, 1] = (
            dense_ref[1 - y, :, c, high, :, cols] + wide(got_core[g, 1 - y, :, high])
        ).astype(jnp.bfloat16)
        second = go(send_one.at[g, 1], got_one.at[g, 1], one_sems, (g, 1), across_y)
        keep_one[g, 0] = dense_ref[:, x, c, low, :, cols] + wide(got_core[g, :, x, low])
        keep_one[g, 1] = dense_ref[y, :, c, high, :, cols] + wide(got_core[g, y, :, high])
        one_copies[g] = (first, second)

    def stage_two(g):
        pair = []
        for h, (side, device) in enumerate(((y, across_y), (x, across_x))):
            one_copies[g][h].wait_recv()
            send_two[g, h] = (keep_one[g, h, 1 - side] + wide(got_one[g, h, 1 - side])).astype(
                jnp.bfloat16
            )
            pair.append(go(send_two.at[g, h], got_two.at[g, h], two_sems, (g, h), device))
            keep_two[g, h * half : (h + 1) * half] = keep_one[g, h, side] + wide(
                got_one[g, h, side]
            )
        two_copies[g] = pair

    def stage_group(g):
        for h in range(2):
            two_copies[g][h].wait_recv()
            part = slice(h * half, (h + 1) * half)
            keep_two[g, part] = keep_two[g, part] + wide(got_two[g, h])
        sent = []
        for d, to in enumerate(groups):
            send_group[g, d] = keep_two[g, to].astype(jnp.bfloat16)
            sent.append(
                go(send_group.at[g, d], got_group.at[g, d], group_sems, (g, d), across_z[d])
            )
        group_copies[g] = sent

    def stage_end(g):
        total = keep_two[g, z]
        for d in range(n_group - 1):
            group_copies[g][d].wait_recv()
            total = total + wide(got_group[g, d])
        total_ref[:, g * width : (g + 1) * width] = total

    weight_copies = [
        go(weight_ref.at[to], got_weight.at[d], weight_sems, (d,), across_z[d])
        for d, to in enumerate(groups)
    ]
    for g in range(chunks):
        stage_core(g)
    stages = (stage_one, stage_two, stage_group, stage_end)
    for step in range(chunks + len(stages) - 1):
        for late, stage in enumerate(stages):
            if 0 <= step - late < chunks:
                stage(step - late)
    total = weight_ref[z]
    for d in range(n_group - 1):
        weight_copies[d].wait_recv()
        total = total + got_weight[d]
    weight_out_ref[...] = total
    for copy in copies:
        copy.wait_send()


def dense_route(dense, weight, n_group):
    columns = dense.shape[-1]
    share = PR // n_group
    half = n_group // 2
    chunks = 4
    width = columns // chunks
    peers = n_group - 1
    vmem = pl.BlockSpec(memory_space=pltpu.VMEM)
    dense = dense.reshape(2, 2, 2, n_group, share, columns)
    weight = jnp.pad(weight.reshape(n_group, 1, share), ((0, 0), (0, 0), (0, LANES - share)))
    weight = jnp.broadcast_to(weight, (n_group, 8, LANES))

    def buffer(*dims, kind=jnp.bfloat16):
        return pltpu.VMEM((chunks,) + dims + (share, width), kind)

    sems = pltpu.SemaphoreType.DMA
    total, weight = pl.pallas_call(
        functools.partial(route_kernel, chunks),
        out_shape=(
            jax.ShapeDtypeStruct((share, columns), jnp.float32),
            jax.ShapeDtypeStruct((8, LANES), jnp.float32),
        ),
        in_specs=[vmem] * 2,
        out_specs=(vmem, vmem),
        scratch_shapes=[
            buffer(2, 2, n_group), buffer(2, 2, n_group),
            buffer(2, 2, half), buffer(2, 2, half), buffer(2, 2, half, kind=jnp.float32),
            buffer(2, half), buffer(2, half), buffer(n_group, kind=jnp.float32),
            buffer(peers), buffer(peers),
            pltpu.VMEM((peers, 8, LANES), jnp.float32),
            sems((2, chunks)), sems((2, chunks, 2)), sems((2, chunks, 2)),
            sems((2, chunks, peers)), sems((2, peers)),
        ],
        compiler_params=pltpu.CompilerParams(
            collective_id=0, has_side_effects=True, vmem_limit_bytes=VMEM_LIMIT
        ),
    )(dense, weight)
    return total, weight[0, :share]


def local(exposures, target_patch, row_offset, basis_index, basis_coef, inv_variance, psf_basis):
    n_patch, n_group = lax.axis_size("patch"), lax.axis_size("vgroup")
    own_patch = lax.axis_index("patch")
    blocks = exposures[0]
    per_device, in_rows, columns = blocks.shape
    taps = psf_basis.shape[-1]
    out_rows = in_rows - taps + 1
    dense = n_patch == 8 and n_group % 2 == 0 and n_patch * PR * columns * 4 <= DENSE_LIMIT

    def own(values):
        return lax.dynamic_slice_in_dim(values, own_patch * per_device, per_device, 0)

    all_starts = target_patch[0, :, 0] * PR + row_offset[0]
    starts, inverse = own(all_starts), own(inv_variance[0])
    picks, coef = own(basis_index[0]).reshape(-1), own(basis_coef[0]).reshape(-1)

    rows = (own_patch * PR + jnp.arange(PR, dtype=jnp.int32))[:, None]
    inside = jnp.logical_and(rows >= all_starts[None], rows < all_starts[None] + out_rows)
    weight = jnp.sum(jnp.where(inside, inv_variance[0][None], 0.0), axis=1)

    result = match_all(blocks, picks, coef, starts, inverse, psf_basis, n_patch, dense)
    if dense:
        numerator, weight = dense_route(result, weight, n_group)
    else:
        targets = target_patch[0, :, 0].reshape(n_patch, per_device)
        own_target = lax.dynamic_slice_in_dim(targets, own_patch, 1, 0)[0]
        numerator = slots_route(
            result, own_target, targets, row_offset[0], inv_variance[0], n_patch, own_patch
        )
        weight = lax.psum_scatter(weight, "vgroup", scatter_dimension=0, tiled=True)
    coadd = jnp.roll(numerator / (1.0 + weight[:, None]), -(LANES // 2), axis=1)
    return (coadd, weight)


def solution(mesh):
    in_specs = (
        P("vgroup", "patch", None, None),
        P("vgroup", None, None),
        P("vgroup", None),
        P("vgroup", None, None),
        P("vgroup", None, None),
        P("vgroup", None),
        P(),
    )
    out_specs = (P(("patch", "vgroup"), None), P(("patch", "vgroup")))
    return jax.shard_map(local, mesh=mesh, in_specs=in_specs, out_specs=out_specs, check_vma=False)
```

```python
import functools

import jax
import jax.numpy as jnp
from jax import lax
from jax.experimental import pallas as pl
from jax.experimental.pallas import tpu as pltpu
from jax.sharding import PartitionSpec as P

PR = 256
LANES = 128
DENSE_LIMIT = 24 * 1024 * 1024
VMEM_LIMIT = 60 * 1024 * 1024


def split_bf16(values):
    high = values.astype(jnp.bfloat16)
    low = (values - high.astype(jnp.float32)).astype(jnp.bfloat16)
    return high, low


def build_tables(basis_ref, down_table, across_table, n_basis, taps):
    half = (taps - 1) // 2
    first = LANES // 2 - half

    def build(b, carry):
        line = basis_ref[b]
        down = pltpu.roll(
            jnp.broadcast_to(line[0:1, :], (32, LANES)), 0, 1, stride=1, stride_axis=0
        )
        down_table[b] = down
        reverse = jnp.broadcast_to(line[1:2, :], (2 * LANES, LANES))
        band = pltpu.roll(reverse, 0, 1, stride=1, stride_axis=0)
        tap = (
            lax.broadcasted_iota(jnp.int32, band.shape, 0)
            - lax.broadcasted_iota(jnp.int32, band.shape, 1)
            - first
        )
        band = jnp.where(jnp.logical_and(tap >= 0, tap < taps), band, 0.0)
        high, low = split_bf16(band)
        across_table[b, :, 0:LANES] = high
        across_table[b, :, LANES : 2 * LANES] = low
        return carry

    lax.fori_loop(0, n_basis, build, 0)


def match_block(b, params_ref, blocks_ref, pixels, windows, down_table, across_table, n_terms):
    in_rows, columns = blocks_ref.shape[1:]
    tiles = columns // LANES
    block = blocks_ref[b]
    pixels[0:in_rows, :] = block
    pixels[64 : 64 + in_rows, :] = block
    picks = [params_ref[t, b].astype(jnp.int32) for t in range(n_terms)]
    rows = jnp.concatenate(
        [params_ref[n_terms + t, b] * down_table[picks[t]] for t in range(n_terms)], axis=0
    )
    rows_high = rows.astype(jnp.bfloat16).astype(jnp.float32)
    lane = lax.broadcasted_iota(jnp.int32, rows.shape, 1)
    taps_down = jnp.where(lane < 64, rows_high, rows - rows_high).astype(jnp.bfloat16)
    for q in range(0, tiles, 2):
        down = jnp.dot(
            taps_down,
            pixels[:, q * LANES : (q + 2) * LANES],
            preferred_element_type=jnp.float32,
        )
        high, low = split_bf16(down)
        for t in range(n_terms):
            for h in range(2):
                for part, offset in ((high, 0), (low, 32)):
                    tile = part[t * 32 : t * 32 + 32, h * LANES : (h + 1) * LANES]
                    right = (q + h) * 64 + offset
                    windows[right : right + 32, (2 * t + 1) * LANES : (2 * t + 2) * LANES] = tile
                    windows[right + 64 : right + 96, 2 * t * LANES : (2 * t + 1) * LANES] = tile
    taps_across = jnp.concatenate([across_table[picks[t]] for t in range(n_terms)], axis=0)
    product = jnp.dot(windows[...], taps_across, preferred_element_type=jnp.float32)
    product = product[:, 0:LANES] + product[:, LANES : 2 * LANES]
    out = [product[c * 64 : c * 64 + 32] + product[c * 64 + 32 : c * 64 + 64] for c in range(tiles + 1)]
    lane = lax.broadcasted_iota(jnp.int32, out[0].shape, 1)
    out[0] = jnp.where(lane < LANES // 2, out[tiles], out[0])
    return jnp.concatenate(out[:tiles], axis=1).astype(jnp.bfloat16)


def match_kernel(
    dense, n_terms, taps,
    params_ref, blocks_hbm, basis_ref, out_ref,
    blocks_ref, pixels, windows, down_table, across_table, load_sem,
):
    count = blocks_ref.shape[0]
    load = pltpu.make_async_copy(blocks_hbm, blocks_ref, load_sem)
    load.start()
    build_tables(basis_ref, down_table, across_table, basis_ref.shape[0], taps)
    pixels[...] = jnp.zeros_like(pixels)
    windows[...] = jnp.zeros_like(windows)
    if dense:
        out_ref[...] = jnp.zeros_like(out_ref)
    load.wait()

    def body(step, carry):
        for k in range(2):
            b = step * 2 + k
            matched = match_block(
                b, params_ref, blocks_ref, pixels.at[k], windows.at[k],
                down_table, across_table, n_terms,
            )
            if dense:
                start = params_ref[2 * n_terms, b].astype(jnp.int32)
                first = jnp.minimum((start // 8) * 8, out_ref.shape[0] - 40)
                row = lax.broadcasted_iota(jnp.int32, (40, 32), 0)
                column = lax.broadcasted_iota(jnp.int32, (40, 32), 1)
                place = (row - column == start - first).astype(jnp.float32).astype(jnp.bfloat16)
                shifted = jnp.dot(place, matched, preferred_element_type=jnp.float32)
                out_ref[pl.ds(pl.multiple_of(first, 8), 40), :] += params_ref[2 * n_terms + 1, b] * shifted
            else:
                out_ref[b] = matched
        return carry

    lax.fori_loop(0, count // 2, body, 0)


def match_all(blocks, params, psf_basis, n_patch, dense):
    count, in_rows, columns = blocks.shape
    n_basis, _, taps = psf_basis.shape
    n_terms = (params.shape[0] - 2) // 2
    half = (taps - 1) // 2
    tiles = columns // LANES
    down_line = jnp.pad(psf_basis[:, 0], ((0, 0), (0, 64 - taps)))
    down_line = jnp.concatenate([down_line, down_line], axis=1)
    tail = LANES - (LANES // 2 - half) - taps + 1
    across_line = jnp.pad(psf_basis[:, 1, ::-1], ((0, 0), (tail, LANES - taps - tail)))
    lines = jnp.stack([down_line, across_line], axis=1)
    if dense:
        out = jax.ShapeDtypeStruct((n_patch * PR, columns), jnp.float32)
    else:
        out = jax.ShapeDtypeStruct((count, in_rows - taps + 1, columns), jnp.bfloat16)
    smem = pl.BlockSpec(memory_space=pltpu.SMEM)
    vmem = pl.BlockSpec(memory_space=pltpu.VMEM)
    return pl.pallas_call(
        functools.partial(match_kernel, dense, n_terms, taps),
        out_shape=out,
        in_specs=[smem, pl.BlockSpec(memory_space=pl.ANY), vmem],
        out_specs=vmem,
        scratch_shapes=[
            pltpu.VMEM(blocks.shape, jnp.bfloat16),
            pltpu.VMEM((2, 128, columns), jnp.bfloat16),
            pltpu.VMEM((2, (tiles + 1) * 64, n_terms * 2 * LANES), jnp.bfloat16),
            pltpu.VMEM((n_basis, 32, LANES), jnp.float32),
            pltpu.VMEM((n_basis, 2 * LANES, 2 * LANES), jnp.bfloat16),
            pltpu.SemaphoreType.DMA,
        ],
        compiler_params=pltpu.CompilerParams(vmem_limit_bytes=VMEM_LIMIT),
    )(params, blocks, lines)


def slots_route(matched, own_target, targets, row_offset, inverse, n_patch, own_patch):
    per_device = matched.shape[0]
    capacity = 2 * per_device // n_patch
    out_rows = matched.shape[1]
    positions = jnp.arange(per_device, dtype=jnp.int32)
    same_patch = targets[:, :, None] == targets[:, None, :]
    earlier = positions[None, :, None] > positions[None, None, :]
    slot_rank = jnp.sum(jnp.logical_and(same_patch, earlier), axis=2)
    peer_ids = jnp.arange(n_patch, dtype=jnp.int32)
    slot_ids = jnp.arange(capacity, dtype=jnp.int32)
    own_rank = lax.dynamic_slice_in_dim(slot_rank, own_patch, 1, 0)[0]
    source_pick = jnp.logical_and(
        own_target[None, None, :] == peer_ids[:, None, None],
        own_rank[None, None, :] == slot_ids[None, :, None],
    )
    source_index = jnp.sum(source_pick * positions[None, None, :], axis=2)
    present = jnp.any(source_pick, axis=2).astype(jnp.bfloat16)[:, :, None, None]
    taking = jnp.logical_and(
        targets[:, None, :] == own_patch, slot_rank[:, None, :] == slot_ids[None, :, None]
    )
    offsets_in = jnp.sum(taking * row_offset.reshape(n_patch, 1, per_device), axis=2)
    weights_in = jnp.sum(taking * inverse.reshape(n_patch, 1, per_device), axis=2)
    outgoing = matched[source_index] * present
    arrived = lax.all_to_all(outgoing, "patch", split_axis=0, concat_axis=0, tiled=True)
    slot_count = n_patch * capacity
    matched = arrived.reshape((slot_count,) + arrived.shape[2:])
    row_index = (
        offsets_in.reshape(slot_count)[:, None] + jnp.arange(out_rows, dtype=jnp.int32)[None, :]
    )
    placement = (row_index[None, :, :] == jnp.arange(PR, dtype=jnp.int32)[:, None, None]).astype(
        jnp.float32
    )
    placement = placement * weights_in.reshape(slot_count)[None, :, None]
    numerator = jnp.einsum(
        "rsi,siw->rw", placement, matched.astype(jnp.float32), precision=lax.Precision.HIGHEST
    )
    return lax.psum_scatter(numerator, "vgroup", scatter_dimension=0, tiled=True)


def route_kernel(
    chunks, dense_hbm, weight_ref, total_ref, weight_out_ref,
    dense_ref, send_core, got_core, send_one, got_one, keep_one, send_two, got_two, keep_two,
    send_group, got_group, got_weight,
    core_sems, one_sems, two_sems, group_sems, weight_sems, load_sems,
):
    p, z = lax.axis_index("patch"), lax.axis_index("vgroup")
    n_group = dense_ref.shape[3]
    half = n_group // 2
    width = dense_ref.shape[-1] // chunks
    y, x, c = p // 4, (p // 2) % 2, p % 2
    across_core = (p + 1 - 2 * c, z)
    across_x = (p + 2 - 4 * x, z)
    across_y = (p + 4 - 8 * y, z)
    groups = [(z + d) % n_group for d in range(1, n_group)]
    across_z = [(p, to) for to in groups]

    loads = []
    for g in range(chunks):
        cols = pl.ds(g * width, width)
        loads.append(
            pltpu.make_async_copy(
                dense_hbm.at[:, :, :, :, :, cols], dense_ref.at[:, :, :, :, :, cols], load_sems.at[g]
            )
        )
        loads[g].start()

    barrier = pltpu.get_barrier_semaphore()
    partners = [across_core, across_x, across_y] + across_z
    for partner in partners:
        pl.semaphore_signal(barrier, inc=1, device_id=partner, device_id_type=pl.DeviceIdType.MESH)
    pl.semaphore_wait(barrier, len(partners))

    copies = []

    def go(source, target, sems, place, device):
        copy = pltpu.make_async_remote_copy(
            src_ref=source, dst_ref=target,
            send_sem=sems.at[(0,) + place], recv_sem=sems.at[(1,) + place],
            device_id=device, device_id_type=pl.DeviceIdType.MESH,
        )
        copy.start()
        copies.append(copy)
        return copy

    def wide(values):
        return values.astype(jnp.float32)

    core_copies, one_copies, two_copies, group_copies = {}, {}, {}, {}

    def stage_core(g):
        cols = slice(g * width, (g + 1) * width)
        loads[g].wait()
        send_core[g] = dense_ref[:, :, 1 - c, :, :, cols].astype(jnp.bfloat16)
        core_copies[g] = go(send_core.at[g], got_core.at[g], core_sems, (g,), across_core)

    def stage_one(g):
        cols = slice(g * width, (g + 1) * width)
        core_copies[g].wait_recv()
        low, high = slice(0, half), slice(half, n_group)
        send_one[g, 0] = (
            dense_ref[:, 1 - x, c, low, :, cols] + wide(got_core[g, :, 1 - x, low])
        ).astype(jnp.bfloat16)
        first = go(send_one.at[g, 0], got_one.at[g, 0], one_sems, (g, 0), across_x)
        send_one[g, 1] = (
            dense_ref[1 - y, :, c, high, :, cols] + wide(got_core[g, 1 - y, :, high])
        ).astype(jnp.bfloat16)
        second = go(send_one.at[g, 1], got_one.at[g, 1], one_sems, (g, 1), across_y)
        keep_one[g, 0] = dense_ref[:, x, c, low, :, cols] + wide(got_core[g, :, x, low])
        keep_one[g, 1] = dense_ref[y, :, c, high, :, cols] + wide(got_core[g, y, :, high])
        one_copies[g] = (first, second)

    def stage_two(g):
        pair = []
        for h, (side, device) in enumerate(((y, across_y), (x, across_x))):
            one_copies[g][h].wait_recv()
            send_two[g, h] = (keep_one[g, h, 1 - side] + wide(got_one[g, h, 1 - side])).astype(
                jnp.bfloat16
            )
            pair.append(go(send_two.at[g, h], got_two.at[g, h], two_sems, (g, h), device))
            keep_two[g, h * half : (h + 1) * half] = keep_one[g, h, side] + wide(
                got_one[g, h, side]
            )
        two_copies[g] = pair

    def stage_group(g):
        for h in range(2):
            two_copies[g][h].wait_recv()
            part = slice(h * half, (h + 1) * half)
            keep_two[g, part] = keep_two[g, part] + wide(got_two[g, h])
        sent = []
        for d, to in enumerate(groups):
            send_group[g, d] = keep_two[g, to].astype(jnp.bfloat16)
            sent.append(
                go(send_group.at[g, d], got_group.at[g, d], group_sems, (g, d), across_z[d])
            )
        group_copies[g] = sent

    def stage_end(g):
        total = keep_two[g, z]
        for d in range(n_group - 1):
            group_copies[g][d].wait_recv()
            total = total + wide(got_group[g, d])
        total_ref[:, g * width : (g + 1) * width] = total

    weight_copies = [
        go(weight_ref.at[to], got_weight.at[d], weight_sems, (d,), across_z[d])
        for d, to in enumerate(groups)
    ]
    for g in range(chunks):
        stage_core(g)
    stages = (stage_one, stage_two, stage_group, stage_end)
    for step in range(chunks + len(stages) - 1):
        for late, stage in enumerate(stages):
            if 0 <= step - late < chunks:
                stage(step - late)
    total = weight_ref[z]
    for d in range(n_group - 1):
        weight_copies[d].wait_recv()
        total = total + got_weight[d]
    weight_out_ref[...] = total
    for copy in copies:
        copy.wait_send()


def dense_route(dense, weight, n_group):
    columns = dense.shape[-1]
    share = PR // n_group
    half = n_group // 2
    chunks = 8
    width = columns // chunks
    peers = n_group - 1
    vmem = pl.BlockSpec(memory_space=pltpu.VMEM)
    dense = dense.reshape(2, 2, 2, n_group, share, columns)
    weight = jnp.pad(weight.reshape(n_group, 1, share), ((0, 0), (0, 0), (0, LANES - share)))
    weight = jnp.broadcast_to(weight, (n_group, 8, LANES))

    def buffer(*dims, kind=jnp.bfloat16):
        return pltpu.VMEM((chunks,) + dims + (share, width), kind)

    sems = pltpu.SemaphoreType.DMA
    total, weight = pl.pallas_call(
        functools.partial(route_kernel, chunks),
        out_shape=(
            jax.ShapeDtypeStruct((share, columns), jnp.float32),
            jax.ShapeDtypeStruct((8, LANES), jnp.float32),
        ),
        in_specs=[pl.BlockSpec(memory_space=pl.ANY), vmem],
        out_specs=(vmem, vmem),
        scratch_shapes=[
            pltpu.VMEM(dense.shape, jnp.float32),
            buffer(2, 2, n_group), buffer(2, 2, n_group),
            buffer(2, 2, half), buffer(2, 2, half), buffer(2, 2, half, kind=jnp.float32),
            buffer(2, half), buffer(2, half), buffer(n_group, kind=jnp.float32),
            buffer(peers), buffer(peers),
            pltpu.VMEM((peers, 8, LANES), jnp.float32),
            sems((2, chunks)), sems((2, chunks, 2)), sems((2, chunks, 2)),
            sems((2, chunks, peers)), sems((2, peers)), sems((chunks,)),
        ],
        compiler_params=pltpu.CompilerParams(
            collective_id=0, has_side_effects=True, vmem_limit_bytes=VMEM_LIMIT
        ),
    )(dense, weight)
    return total, weight[0, :share]


def local(exposures, target_patch, row_offset, basis_index, basis_coef, inv_variance, psf_basis):
    n_patch, n_group = lax.axis_size("patch"), lax.axis_size("vgroup")
    own_patch = lax.axis_index("patch")
    blocks = exposures[0]
    per_device, in_rows, columns = blocks.shape
    taps = psf_basis.shape[-1]
    out_rows = in_rows - taps + 1
    dense = n_patch == 8 and n_group % 2 == 0 and n_patch * PR * columns * 4 <= DENSE_LIMIT

    all_starts = target_patch[0, :, 0] * PR + row_offset[0]
    params = jnp.concatenate(
        [
            basis_index[0].T.astype(jnp.float32),
            basis_coef[0].T,
            all_starts.astype(jnp.float32)[None],
            inv_variance,
        ],
        axis=0,
    )
    params = lax.dynamic_slice_in_dim(params, own_patch * per_device, per_device, 1)

    rows = (own_patch * PR + jnp.arange(PR, dtype=jnp.int32))[:, None]
    inside = jnp.logical_and(rows >= all_starts[None], rows < all_starts[None] + out_rows)
    weight = jnp.sum(jnp.where(inside, inv_variance[0][None], 0.0), axis=1)

    result = match_all(blocks, params, psf_basis, n_patch, dense)
    if dense:
        numerator, weight = dense_route(result, weight, n_group)
    else:
        targets = target_patch[0, :, 0].reshape(n_patch, per_device)
        own_target = lax.dynamic_slice_in_dim(targets, own_patch, 1, 0)[0]
        numerator = slots_route(
            result, own_target, targets, row_offset[0], inv_variance[0], n_patch, own_patch
        )
        weight = lax.psum_scatter(weight, "vgroup", scatter_dimension=0, tiled=True)
    coadd = jnp.roll(numerator / (1.0 + weight[:, None]), -(LANES // 2), axis=1)
    return (coadd, weight)


def solution(mesh):
    in_specs = (
        P("vgroup", "patch", None, None),
        P("vgroup", None, None),
        P("vgroup", None),
        P("vgroup", None, None),
        P("vgroup", None, None),
        P("vgroup", None),
        P(),
    )
    out_specs = (P(("patch", "vgroup"), None), P(("patch", "vgroup")))
    return jax.shard_map(local, mesh=mesh, in_specs=in_specs, out_specs=out_specs, check_vma=False)
```
